512 devices in a mesh: row: 16 (over z), col: 32 (over y, x, core).
Axes of the slice: x: 4, y: 4, z: 16, core: 2. Of those that a mesh axis runs over, the one named last changes fastest.
Arguments:
- matrix: float32 [4, 4096, 2, 8192], P(None, 'row', None, 'col'), may hold values from -6 to 6, as said below
Outputs:
- factored: float32 [4, 4096, 2, 8192], P(None, 'row', None, 'col')
The draws below stay inside these ranges and needn't reach their ends.
Inputs may be any that keep to these rules, and one draw needn't show every extreme that they name: symmetric; the leading 2 * 256 rows and columns form a positive definite matrix.
All inputs are finite; a program needn't handle non-finite values.
Results may differ from the reference program's by a relative error of at most 0.0001.
Values sent between devices are 32-bit elements; how exact they have to be, the bound alone decides.
No kernel may reach another device: no remote copies, remote signals or barrier semaphores. Data moves between devices by JAX's collectives and lax.ppermute only.
A program may use at most 64 MiB of HBM per device.

```python
import jax
import jax.numpy as jnp
from jax import lax

B = 256
BC = 2
PANELS = 2
BR = 4
ORDER = 16384
N_ROW = 16
N_COL = 32


def draw_matrix(key, part):
    first_key, second_key = jax.random.split(key)
    leading = PANELS * B
    base = jnp.clip(jax.random.normal(first_key, (ORDER, ORDER), jnp.float32), -6.0, 6.0)
    sym = (base + base.T) * 0.5
    index = jnp.arange(ORDER)
    inner = index < leading
    both_in = inner[:, None] & inner[None, :]
    both_out = (~inner)[:, None] & (~inner)[None, :]
    diag_values = 2.0 + 2.0 * jax.random.uniform(second_key, (ORDER,), jnp.float32)
    lead_part = 1.9 / leading * jnp.tanh(sym)
    trailing = sym
    result = jnp.where(both_in, lead_part, jnp.where(both_out, trailing, 0.25 * sym))
    on_diag = (index[:, None] == index[None, :]) & both_in
    result = jnp.where(on_diag, diag_values[None, :], result)
    return result.astype(jnp.float32).reshape(BR, N_ROW * B, BC, N_COL * B)


def setup_inputs(seed: int = 0) -> dict:
    seeds = jax.random.split(jax.random.key(seed), 2)
    return {
        "matrix": draw_matrix(jax.random.fold_in(seeds[1], 71), 0),
    }


def reference(matrix):
    full = matrix.reshape(ORDER, ORDER)
    for panel in range(PANELS):
        start = panel * B
        stop = start + B
        diag_factor = jnp.linalg.cholesky(full[start:stop, start:stop])
        below = lax.linalg.triangular_solve(diag_factor, full[stop:, start:stop], left_side=False, lower=True, transpose_a=True)
        trailing = full[stop:, stop:] - jnp.dot(below.astype(jnp.float32), below.T.astype(jnp.float32), precision=lax.Precision.HIGHEST, preferred_element_type=jnp.float32)
        column = jnp.concatenate((jnp.zeros((start, B), jnp.float32), diag_factor, below), axis=0)
        full = full.at[:, start:stop].set(column)
        full = full.at[start:stop, stop:].set(jnp.zeros((B, ORDER - stop), jnp.float32))
        full = full.at[stop:, stop:].set(trailing)
    return full.reshape(BR, N_ROW * B, BC, N_COL * B)
```

```python
import jax
import jax.numpy as jnp
from jax import lax
from jax.experimental import pallas as pl
from jax.experimental.pallas import tpu as pltpu
from jax.sharding import PartitionSpec as P

HI = lax.Precision.HIGHEST
TILE = 128
STEP = 8
NZ, NY, NX, NC = 16, 4, 4, 2
NCOL = NY * NX * NC
TILES = (((0, 0), (1, 0), (1, 1), (2, 0), (2, 1)), ((2, 2), (3, 2), (3, 3), (3, 0), (3, 1)))
HALF = len(TILES[0])


def dot(a, b, ca, cb):
    dims = (((ca,), (cb,)), ((), ()))
    return lax.dot_general(a, b, dims, precision=HI, preferred_element_type=jnp.float32)


def factor_tile(work):
    lane = lax.broadcasted_iota(jnp.int32, (STEP, 2 * TILE), 1)
    sub = lax.broadcasted_iota(jnp.int32, (STEP, 2 * TILE), 0)
    for start in range(0, TILE, STEP):
        stop = start + STEP
        rows = work[start:stop, :]
        done = jnp.zeros_like(rows)
        for j in range(STEP):
            column = rows[:, start + j : start + j + 1]
            scale = lax.rsqrt(column[j : j + 1, :])
            row = rows[j : j + 1, :] * scale
            rows = rows - (column * scale) * row
            done = jnp.where(sub == j, row, done)
        done = jnp.where(lane >= start + sub, done, 0.0)
        work[start:stop, :] = done
        if stop < TILE:
            work[stop:, :] = work[stop:, :] - dot(done[:, stop:TILE], done, 0, 0)


def factor_kernel(first, second, inv, a, work):
    n = inv.shape[0]
    for block, places in zip((first, second), TILES):
        for t, (i, j) in enumerate(places):
            a[i * TILE : (i + 1) * TILE, j * TILE : (j + 1) * TILE] = block[t]
    ri = lax.broadcasted_iota(jnp.int32, (TILE, TILE), 0)
    ci = lax.broadcasted_iota(jnp.int32, (TILE, TILE), 1)
    eye = jnp.where(ri == ci, 1.0, 0.0)
    inv[...] = jnp.zeros_like(inv)
    for s in range(0, n, TILE):
        e = s + TILE
        work[:, :TILE] = a[s:e, s:e]
        work[:, TILE:] = eye
        factor_tile(work)
        tile_inv = work[:, TILE:]
        if s:
            inv[s:e, 0:s] = dot(tile_inv, inv[s:e, 0:s], 1, 0)
        inv[s:e, s:e] = tile_inv
        if e < n:
            panel = dot(a[e:, s:e], tile_inv, 1, 1)
            for r in range(e, n, TILE):
                rows = panel[r - e : r - e + TILE]
                a[r : r + TILE, e : r + TILE] = a[r : r + TILE, e : r + TILE] - dot(
                    rows, panel[: r - e + TILE], 1, 1
                )
            inv[e:, 0:e] = inv[e:, 0:e] - dot(panel, inv[s:e, 0:e], 1, 0)


def factor(first, second):
    n = 4 * TILE
    vmem = pl.BlockSpec(memory_space=pltpu.VMEM)
    return pl.pallas_call(
        factor_kernel,
        out_shape=jax.ShapeDtypeStruct((n, n), jnp.float32),
        in_specs=[vmem] * 2,
        out_specs=vmem,
        scratch_shapes=[pltpu.VMEM((n, n), jnp.float32), pltpu.VMEM((TILE, 2 * TILE), jnp.float32)],
        compiler_params=pltpu.CompilerParams(vmem_limit_bytes=24 * 1024 * 1024),
        cost_estimate=pl.CostEstimate(flops=30_000_000_000, bytes_accessed=2_000_000, transcendentals=0),
    )(first, second)


def device(z, y, x, c):
    return (((z % NZ) * NY + y % NY) * NX + x % NX) * NC + c


def send(block, pairs):
    return lax.ppermute(block, ("row", "col"), pairs)


def only(mask, block):
    return jnp.where(mask, block, jnp.zeros_like(block))


def plane(pairs):
    return [(device(z, *s, c), device(z, *t, c)) for z in range(NZ) for s, t in pairs for c in range(NC)]


def spread_rows(block):
    first, second = block[:2], block[2:]
    for k in (2, 1):
        spots = range(0, NY, 2 * k)
        first += send(first, plane([((y, 0), (y + k, 0)) for y in spots]))
        second += send(second, plane([((0, x), (0, x + k)) for x in spots]))
    for k in (2, 1):
        spots = range(0, NY, 2 * k)
        first += send(first, plane([((y, x), (y, x + k)) for y in range(NY) for x in spots]))
        second += send(second, plane([((y, x), (y + k, x)) for y in spots for x in range(NX)]))
    return jnp.concatenate((first, second))


RING = (
    (((0, 11, 0), (1, 6, 1)), ((0, 1, 0), (1, 0, 1))),
    (((0, 11, 1), (1, 6, 0), (11, 14, 0), (6, 3, 1)), ((11, 9, 0), (6, 8, 1))),
    (
        ((0, 14, 1), (14, 15, 0), (9, 10, 0), (8, 9, 1), (11, 12, 0), (1, 3, 0), (3, 2, 1), (6, 7, 0)),
        ((14, 13, 0), (9, 8, 0), (8, 7, 1), (11, 10, 1), (3, 4, 1), (6, 5, 0)),
    ),
    (((0, 15, 1), (14, 13, 1), (11, 12, 1), (1, 2, 0), (3, 4, 0), (6, 5, 1)),),
)


def spread_cols(top, low, row):
    for step in RING:
        got = []
        for moves in step:
            sends_low = jnp.zeros((), bool)
            takes_top = jnp.zeros((), bool)
            for source, target, panel in moves:
                sends_low |= (row == source) & (panel == 1)
                takes_top |= (row == target) & (panel == 0)
            pairs = [(s * NCOL + j, t * NCOL + j) for s, t, _ in moves for j in range(NCOL)]
            got.append((takes_top, send(jnp.where(sends_low, low, top), pairs)))
        for takes_top, block in got:
            top = top + only(takes_top, block)
            low = low + only(~takes_top, block)
    return top, low


def tree():
    along = {"z": lambda h, k: (h[0] + k, h[1], h[2]), "y": lambda h, k: (h[0], h[1] + k, h[2])}
    along["x"] = lambda h, k: (h[0], h[1], h[2] + k)
    far, near, side = ("z", (8, 4, 12)), ("z", (2, 1, 15)), (2, 1, 3)
    orders = ((far, near, ("y", side), ("x", side)), (("y", side), ("x", side), far, near))
    held = [[(0, 0, 0)], [(1, 0, 0)]]
    levels = []
    for level in range(4):
        sets = [[], [], []]
        for half, order in enumerate(orders):
            axis, offsets = order[level]
            new = []
            for n, k in enumerate(offsets):
                for h in held[half]:
                    t = along[axis](h, k)
                    sets[n].append((device(*h, half), device(*t, half)))
                    new.append(t)
            held[half] = held[half] + new
        levels.append(sets)
    return levels


CHIPS = [(z, y, x) for z in range(NZ) for y in range(NY) for x in range(NX)]


SWAP = [(device(*h, c), device(*h, 1 - c)) for h in CHIPS for c in range(NC)]


def shards(matrix):
    row = lax.axis_index("row")
    col = lax.axis_index("col")
    me = row * NCOL + col
    core = col % NC
    a_count, width, c_count, _ = matrix.shape

    with jax.named_scope("spread_diagonal"):
        corner = matrix[0, :, 0, :]
        upper, lower = corner[:TILE], corner[TILE:]
        roots = device(0, 0, 0, 0), device(1, 0, 0, 1)
        across = device(1, 0, 0, 0)
        beside = jnp.stack((upper[:, :TILE], upper[:, TILE:])), jnp.stack((lower[:, :TILE], lower[:, TILE:]))
        got = send(beside[0], [(across, roots[0])]) + send(beside[1], [(across, roots[1])])
        half = jnp.concatenate((jnp.stack((upper[:, :TILE], lower[:, :TILE], lower[:, TILE:])), got))
        half = only((me == roots[0]) | (me == roots[1]), half)
        for sets in tree():
            got = [send(half, pairs) for pairs in sets]
            half = half + (got[0] + got[1] + got[2])
        other = send(half, SWAP)
        first = jnp.where(core == 0, half, other)
        second = jnp.where(core == 0, other, half)
    with jax.named_scope("factor_diagonal"):
        inverse = factor(first, second)
    with jax.named_scope("spread_rows"):
        mine = spread_rows(only(col < NC, matrix[:, :, 0, :]))
        other = send(mine, SWAP)
        left = jnp.where(core == 1, other, mine)
        right = jnp.where(core == 1, mine, other)
    with jax.named_scope("spread_cols"):
        top, low = spread_cols(only(row == 0, matrix[0]), only(row == 1, matrix[0]), row)
    with jax.named_scope("update"):
        left = left.reshape(a_count * width, width)
        right = right.reshape(a_count * width, width)
        cols = jnp.concatenate((top, low)).reshape(2 * width, c_count * width)
        head = dot(left, inverse[:width, :width], 1, 1)
        tail = dot(left, inverse[width:, :width], 1, 1) + dot(right, inverse[width:, width:], 1, 1)
        solved_cols = dot(inverse, cols, 1, 0)
        product = dot(jnp.concatenate((head, tail), 1), solved_cols, 1, 0)
        product = product.reshape(a_count, width, c_count, width)
        row_ids = (jnp.arange(a_count, dtype=jnp.int32) * NZ + row)[:, None, None]
        col_ids = (jnp.arange(c_count, dtype=jnp.int32) * NCOL + col)[None, None, :, None]
        p = lax.broadcasted_iota(jnp.int32, (1, width, width), 1)
        q = lax.broadcasted_iota(jnp.int32, (1, width, width), 2)
        lower = p >= q
        head = head.reshape(a_count, width, width)
        tail = tail.reshape(a_count, width, width)
        head = jnp.where((row_ids > 0) | lower, head, 0.0)
        tail = jnp.where((row_ids > 1) | ((row_ids == 1) & lower), tail, 0.0)
        trailing = jnp.where(row_ids[..., None] > 1, matrix - product, 0.0)
        return jnp.where(
            col_ids == 0, head[:, :, None, :], jnp.where(col_ids == 1, tail[:, :, None, :], trailing)
        )


def solution(mesh):
    spec = (P(None, "row", None, "col"),)
    return jax.shard_map(shards, mesh=mesh, in_specs=spec, out_specs=spec[0], check_vma=False)
```

```python
import jax
import jax.numpy as jnp
from jax import lax
from jax.experimental import pallas as pl
from jax.experimental.pallas import tpu as pltpu
from jax.sharding import PartitionSpec as P

HI = lax.Precision.HIGHEST
TILE = 128
STEP = 32
SUB = 16
NZ, NY, NX, NC = 16, 4, 4, 2
NCOL = NY * NX * NC
TILES = (((0, 0), (1, 0), (1, 1), (2, 0), (2, 1)), ((2, 2), (3, 2), (3, 3), (3, 0), (3, 1)))
HALF = len(TILES[0])


def dot(a, b, ca, cb):
    dims = (((ca,), (cb,)), ((), ()))
    return lax.dot_general(a, b, dims, precision=HI, preferred_element_type=jnp.float32)


def factor_tile(work):
    lane = lax.broadcasted_iota(jnp.int32, (SUB, 2 * TILE), 1)
    sub = lax.broadcasted_iota(jnp.int32, (SUB, 2 * TILE), 0)
    for start in range(0, TILE, STEP):
        stop = start + STEP
        parts = [work[s : s + SUB, :] for s in range(start, stop, SUB)]
        for p in range(STEP // SUB):
            first = start + p * SUB
            rows = parts[p]
            columns = [jnp.broadcast_to(rows[:, first + j : first + j + 1], (SUB, TILE)) for j in range(SUB)]
            below = [
                [jnp.broadcast_to(r[:, first + j : first + j + 1], (SUB, TILE)) for j in range(SUB)]
                for r in parts[p + 1 :]
            ]
            done = jnp.zeros_like(rows)
            for j in range(SUB):
                scale = lax.rsqrt(columns[j][j : j + 1, :])
                weight = columns[j] * scale
                row = rows[j : j + 1, :] * jnp.concatenate((scale, scale), 1)
                rows = rows - jnp.concatenate((weight, weight), 1) * row
                for t, cols in enumerate(below):
                    w = cols[j] * scale
                    parts[p + 1 + t] = parts[p + 1 + t] - jnp.concatenate((w, w), 1) * row
                    for i in range(j + 1, SUB):
                        cols[i] = cols[i] - w * (columns[i][j : j + 1, :] * scale)
                for i in range(j + 1, SUB):
                    columns[i] = columns[i] - weight * (columns[i][j : j + 1, :] * scale)
                done = jnp.where(sub == j, row, done)
            parts[p] = jnp.where(lane >= first + sub, done, 0.0)
        done = jnp.concatenate(parts)
        work[start:stop, :] = done
        if stop < TILE:
            work[stop:, :] = work[stop:, :] - dot(done[:, stop:TILE], done, 0, 0)


def factor_kernel(first, second, inv, a, work):
    n = inv.shape[0]
    for block, places in zip((first, second), TILES):
        for t, (i, j) in enumerate(places):
            a[i * TILE : (i + 1) * TILE, j * TILE : (j + 1) * TILE] = block[t]
    ri = lax.broadcasted_iota(jnp.int32, (TILE, TILE), 0)
    ci = lax.broadcasted_iota(jnp.int32, (TILE, TILE), 1)
    eye = jnp.where(ri == ci, 1.0, 0.0)
    inv[...] = jnp.zeros_like(inv)
    for s in range(0, n, TILE):
        e = s + TILE
        work[:, :TILE] = a[s:e, s:e]
        work[:, TILE:] = eye
        factor_tile(work)
        tile_inv = work[:, TILE:]
        if s:
            inv[s:e, 0:s] = dot(tile_inv, inv[s:e, 0:s], 1, 0)
        inv[s:e, s:e] = tile_inv
        if e < n:
            panel = dot(a[e:, s:e], tile_inv, 1, 1)
            for r in range(e, n, TILE):
                rows = panel[r - e : r - e + TILE]
                a[r : r + TILE, e : r + TILE] = a[r : r + TILE, e : r + TILE] - dot(
                    rows, panel[: r - e + TILE], 1, 1
                )
            inv[e:, 0:e] = inv[e:, 0:e] - dot(panel, inv[s:e, 0:e], 1, 0)


def factor(first, second):
    n = 4 * TILE
    vmem = pl.BlockSpec(memory_space=pltpu.VMEM)
    return pl.pallas_call(
        factor_kernel,
        out_shape=jax.ShapeDtypeStruct((n, n), jnp.float32),
        in_specs=[vmem] * 2,
        out_specs=vmem,
        scratch_shapes=[pltpu.VMEM((n, n), jnp.float32), pltpu.VMEM((TILE, 2 * TILE), jnp.float32)],
        compiler_params=pltpu.CompilerParams(vmem_limit_bytes=24 * 1024 * 1024),
        cost_estimate=pl.CostEstimate(flops=30_000_000_000, bytes_accessed=2_000_000, transcendentals=0),
    )(first, second)


def device(z, y, x, c):
    return (((z % NZ) * NY + y % NY) * NX + x % NX) * NC + c


def send(block, pairs):
    return lax.ppermute(block, ("row", "col"), pairs)


def only(mask, block):
    return jnp.where(mask, block, jnp.zeros_like(block))


def plane(pairs):
    return [(device(z, *s, c), device(z, *t, c)) for z in range(NZ) for s, t in pairs for c in range(NC)]


def spread_rows(step, first, second, y, x):
    k = (2, 1, 2, 1)[step]
    spots = range(0, NY, 2 * k)
    if step < 2:
        to_first = send(first, plane([((y, 0), (y + k, 0)) for y in spots]))
        to_second = send(second, plane([((0, x), (0, x + k)) for x in spots]))
    else:
        to_first = send(first, plane([((y, x), (y, x + k)) for y in range(NY) for x in spots]))
        to_second = send(second, plane([((y, x), (y + k, x)) for y in spots for x in range(NX)]))
    lead, other = (y, x), (x, y)
    at = [(m if step < 2 else n) % (2 * k) == k for m, n in (lead, other)]
    if step < 2:
        at = [at[0] & (x == 0), at[1] & (y == 0)]
    return jnp.where(at[0], to_first, first), jnp.where(at[1], to_second, second)


RING = (
    (((0, 11, 0), (1, 6, 1)), ((0, 1, 0), (1, 0, 1))),
    (((0, 11, 1), (1, 6, 0), (11, 14, 0), (6, 3, 1)), ((11, 9, 0), (6, 8, 1))),
    (
        ((0, 14, 1), (14, 15, 0), (9, 10, 0), (8, 9, 1), (11, 12, 0), (1, 3, 0), (3, 2, 1), (6, 7, 0)),
        ((14, 13, 0), (9, 8, 0), (8, 7, 1), (11, 10, 1), (3, 4, 1), (6, 5, 0)),
    ),
    (((0, 15, 1), (14, 13, 1), (11, 12, 1), (1, 2, 0), (3, 4, 0), (6, 5, 1)),),
)


def among(index, values):
    found = jnp.zeros((), bool)
    for value in values:
        found |= index == value
    return found


def spread_cols(step, top, low, row):
    got = []
    for moves in RING[step]:
        sends_low = among(row, [s for s, _, panel in moves if panel == 1])
        pairs = [(s * NCOL + j, t * NCOL + j) for s, t, _ in moves for j in range(NCOL)]
        got.append(send(jnp.where(sends_low, low, top), pairs))
    for moves, block in zip(RING[step], got):
        top = jnp.where(among(row, [t for _, t, panel in moves if panel == 0]), block, top)
        low = jnp.where(among(row, [t for _, t, panel in moves if panel == 1]), block, low)
    return top, low


def tree():
    along = {"z": lambda h, k: (h[0] + k, h[1], h[2]), "y": lambda h, k: (h[0], h[1] + k, h[2])}
    along["x"] = lambda h, k: (h[0], h[1], h[2] + k)
    far, near, side = ("z", (8, 4, 12)), ("z", (2, 1, 15)), (2, 1, 3)
    orders = ((far, near, ("y", side), ("x", side)), (("y", side), ("x", side), far, near))
    held = [[(0, 0, 0)], [(1, 0, 0)]]
    levels = []
    for level in range(4):
        sets = [[], [], []]
        for half, order in enumerate(orders):
            axis, offsets = order[level]
            new = []
            for n, k in enumerate(offsets):
                for h in held[half]:
                    t = along[axis](h, k)
                    sets[n].append((device(*h, half), device(*t, half)))
                    new.append(t)
            held[half] = held[half] + new
        levels.append(sets)
    return levels


CHIPS = [(z, y, x) for z in range(NZ) for y in range(NY) for x in range(NX)]


SWAP = [(device(*h, c), device(*h, 1 - c)) for h in CHIPS for c in range(NC)]


def shards(matrix):
    row = lax.axis_index("row")
    col = lax.axis_index("col")
    me = row * NCOL + col
    core = col % NC
    a_count, width, c_count, _ = matrix.shape

    y, x = col // (NX * NC), col // NC % NX
    hold = lax.optimization_barrier

    def step_panels(step, state):
        with jax.named_scope("spread_panels"):
            first, second, top, low = state
            return spread_rows(step, first, second, y, x) + spread_cols(step, top, low, row)

    def step_diagonal(half, sets):
        with jax.named_scope("spread_diagonal"):
            got = [send(half, pairs) for pairs in sets]
            return half + (got[0] + got[1] + got[2])

    panels = matrix[:2, :, 0, :], matrix[2:, :, 0, :], matrix[0], matrix[0]
    with jax.named_scope("spread_diagonal"):
        corner = matrix[0, :, 0, :]
        upper, lower = corner[:TILE], corner[TILE:]
        roots = device(0, 0, 0, 0), device(1, 0, 0, 1)
        across = device(1, 0, 0, 0)
        beside = jnp.stack((upper[:, :TILE], upper[:, TILE:])), jnp.stack((lower[:, :TILE], lower[:, TILE:]))
        got = send(beside[0], [(across, roots[0])]) + send(beside[1], [(across, roots[1])])
        half = jnp.concatenate((jnp.stack((upper[:, :TILE], lower[:, :TILE], lower[:, TILE:])), got))
        half = only((me == roots[0]) | (me == roots[1]), half)
    levels = tree()
    half, panels = hold((step_diagonal(half, levels[0]), step_panels(0, panels)))
    half = step_diagonal(step_diagonal(half, levels[1]), levels[2])
    half, panels = hold((half, step_panels(1, panels)))
    half = step_diagonal(half, levels[3])
    with jax.named_scope("spread_diagonal"):
        other = send(half, SWAP)
        diagonal = jnp.where(core == 0, half, other), jnp.where(core == 0, other, half)
    diagonal, panels = hold((diagonal, step_panels(2, panels)))
    with jax.named_scope("factor_diagonal"):
        inverse = factor(*diagonal)
    inverse, (first, second, top, low) = hold((inverse, step_panels(3, panels)))
    with jax.named_scope("spread_panels"):
        mine = jnp.concatenate((first, second))
        other = send(mine, SWAP)
        left = jnp.where(core == 1, other, mine)
        right = jnp.where(core == 1, mine, other)
    with jax.named_scope("update"):
        left = left.reshape(a_count * width, width)
        right = right.reshape(a_count * width, width)
        cols = jnp.concatenate((top, low))
        head = dot(left, inverse[:width, :width], 1, 1)
        tail = dot(left, inverse[width:, :width], 1, 1) + dot(right, inverse[width:, width:], 1, 1)
        rows = jnp.concatenate((head, tail), 1).reshape(a_count, width, 2 * width)
        solved = dot(inverse, cols.reshape(2 * width, c_count * width), 1, 0)
        solved = solved.reshape(2 * width, c_count, width)
        product = jnp.einsum("apk,kcq->apcq", rows, solved, precision=HI)
        row_ids = (jnp.arange(a_count, dtype=jnp.int32) * NZ + row)[:, None, None]
        col_ids = (jnp.arange(c_count, dtype=jnp.int32) * NCOL + col)[None, None, :, None]
        p = lax.broadcasted_iota(jnp.int32, (1, width, width), 1)
        q = lax.broadcasted_iota(jnp.int32, (1, width, width), 2)
        lower = p >= q
        head = head.reshape(a_count, width, width)
        tail = tail.reshape(a_count, width, width)
        head = jnp.where((row_ids > 0) | lower, head, 0.0)
        tail = jnp.where((row_ids > 1) | ((row_ids == 1) & lower), tail, 0.0)
        trailing = jnp.where(row_ids[..., None] > 1, matrix - product, 0.0)
        return jnp.where(
            col_ids == 0, head[:, :, None, :], jnp.where(col_ids == 1, tail[:, :, None, :], trailing)
        )


def solution(mesh):
    spec = (P(None, "row", None, "col"),)
    return jax.shard_map(shards, mesh=mesh, in_specs=spec, out_specs=spec[0], check_vma=False)
```

```python
import jax
import jax.numpy as jnp
from jax import lax
from jax.experimental import pallas as pl
from jax.experimental.pallas import tpu as pltpu
from jax.sharding import PartitionSpec as P

HI = lax.Precision.HIGHEST
TILE = 128
STEP = 32
SUB = 16
NZ, NY, NX, NC = 16, 4, 4, 2
NCOL = NY * NX * NC
TILES = (((0, 0), (1, 0), (1, 1), (2, 0), (2, 1)), ((2, 2), (3, 2), (3, 3), (3, 0), (3, 1)))
HALF = len(TILES[0])


def dot(a, b, ca, cb):
    dims = (((ca,), (cb,)), ((), ()))
    return lax.dot_general(a, b, dims, precision=HI, preferred_element_type=jnp.float32)


def factor_tile(work):
    lane = lax.broadcasted_iota(jnp.int32, (SUB, 2 * TILE), 1)
    sub = lax.broadcasted_iota(jnp.int32, (SUB, 2 * TILE), 0)
    for start in range(0, TILE, STEP):
        stop = start + STEP
        parts = [work[s : s + SUB, :] for s in range(start, stop, SUB)]
        for p in range(STEP // SUB):
            first = start + p * SUB
            rows = parts[p]
            columns = [jnp.broadcast_to(rows[:, first + j : first + j + 1], (SUB, TILE)) for j in range(SUB)]
            below = [
                [jnp.broadcast_to(r[:, first + j : first + j + 1], (SUB, TILE)) for j in range(SUB)]
                for r in parts[p + 1 :]
            ]
            done = jnp.zeros_like(rows)
            for j in range(SUB):
                scale = lax.rsqrt(columns[j][j : j + 1, :])
                weight = columns[j] * scale
                row = rows[j : j + 1, :] * jnp.concatenate((scale, scale), 1)
                rows = rows - jnp.concatenate((weight, weight), 1) * row
                for t, cols in enumerate(below):
                    w = cols[j] * scale
                    parts[p + 1 + t] = parts[p + 1 + t] - jnp.concatenate((w, w), 1) * row
                    for i in range(j + 1, SUB):
                        cols[i] = cols[i] - w * (columns[i][j : j + 1, :] * scale)
                for i in range(j + 1, SUB):
                    columns[i] = columns[i] - weight * (columns[i][j : j + 1, :] * scale)
                done = jnp.where(sub == j, row, done)
            parts[p] = jnp.where(lane >= first + sub, done, 0.0)
        done = jnp.concatenate(parts)
        work[start:stop, :] = done
        if stop < TILE:
            work[stop:, :] = work[stop:, :] - dot(done[:, stop:TILE], done, 0, 0)


def factor_kernel(first, second, inv, a, work):
    n = inv.shape[0]
    for block, places in zip((first, second), TILES):
        for t, (i, j) in enumerate(places):
            a[i * TILE : (i + 1) * TILE, j * TILE : (j + 1) * TILE] = block[t]
    ri = lax.broadcasted_iota(jnp.int32, (TILE, TILE), 0)
    ci = lax.broadcasted_iota(jnp.int32, (TILE, TILE), 1)
    eye = jnp.where(ri == ci, 1.0, 0.0)
    inv[...] = jnp.zeros_like(inv)
    for s in range(0, n, TILE):
        e = s + TILE
        work[:, :TILE] = a[s:e, s:e]
        work[:, TILE:] = eye
        factor_tile(work)
        tile_inv = work[:, TILE:]
        if s:
            inv[s:e, 0:s] = dot(tile_inv, inv[s:e, 0:s], 1, 0)
        inv[s:e, s:e] = tile_inv
        if e < n:
            panel = dot(a[e:, s:e], tile_inv, 1, 1)
            for r in range(e, n, TILE):
                rows = panel[r - e : r - e + TILE]
                a[r : r + TILE, e : r + TILE] = a[r : r + TILE, e : r + TILE] - dot(
                    rows, panel[: r - e + TILE], 1, 1
                )
            inv[e:, 0:e] = inv[e:, 0:e] - dot(panel, inv[s:e, 0:e], 1, 0)


def factor(first, second):
    n = 4 * TILE
    vmem = pl.BlockSpec(memory_space=pltpu.VMEM)
    return pl.pallas_call(
        factor_kernel,
        out_shape=jax.ShapeDtypeStruct((n, n), jnp.float32),
        in_specs=[vmem] * 2,
        out_specs=vmem,
        scratch_shapes=[pltpu.VMEM((n, n), jnp.float32), pltpu.VMEM((TILE, 2 * TILE), jnp.float32)],
        compiler_params=pltpu.CompilerParams(vmem_limit_bytes=24 * 1024 * 1024),
        cost_estimate=pl.CostEstimate(flops=30_000_000_000, bytes_accessed=2_000_000, transcendentals=0),
    )(first, second)


def device(z, y, x, c):
    return (((z % NZ) * NY + y % NY) * NX + x % NX) * NC + c


def send(block, pairs):
    return lax.ppermute(block, ("row", "col"), pairs)


def only(mask, block):
    return jnp.where(mask, block, jnp.zeros_like(block))


def plane(pairs):
    return [(device(z, *s, c), device(z, *t, c)) for z in range(NZ) for s, t in pairs for c in range(NC)]


def spread_rows(step, first, second, y, x):
    k = (2, 1, 2, 1)[step]
    spots = range(0, NY, 2 * k)
    if step < 2:
        to_first = send(first, plane([((y, 0), (y + k, 0)) for y in spots]))
        to_second = send(second, plane([((0, x), (0, x + k)) for x in spots]))
    else:
        to_first = send(first, plane([((y, x), (y, x + k)) for y in range(NY) for x in spots]))
        to_second = send(second, plane([((y, x), (y + k, x)) for y in spots for x in range(NX)]))
    lead, other = (y, x), (x, y)
    at = [(m if step < 2 else n) % (2 * k) == k for m, n in (lead, other)]
    if step < 2:
        at = [at[0] & (x == 0), at[1] & (y == 0)]
    return jnp.where(at[0], to_first, first), jnp.where(at[1], to_second, second)


RING = (
    (((0, 11, 0), (1, 6, 1)), ((0, 1, 0), (1, 0, 1))),
    (((0, 11, 1), (1, 6, 0), (11, 14, 0), (6, 3, 1)), ((11, 9, 0), (6, 8, 1))),
    (
        ((0, 14, 1), (14, 15, 0), (9, 10, 0), (8, 9, 1), (11, 12, 0), (1, 3, 0), (3, 2, 1), (6, 7, 0)),
        ((14, 13, 0), (9, 8, 0), (8, 7, 1), (11, 10, 1), (3, 4, 1), (6, 5, 0)),
    ),
    (((0, 15, 1), (14, 13, 1), (11, 12, 1), (1, 2, 0), (3, 4, 0), (6, 5, 1)),),
)


def among(index, values):
    found = jnp.zeros((), bool)
    for value in values:
        found |= index == value
    return found


def spread_cols(step, top, low, row):
    got = []
    for moves in RING[step]:
        sends_low = among(row, [s for s, _, panel in moves if panel == 1])
        pairs = [(s * NCOL + j, t * NCOL + j) for s, t, _ in moves for j in range(NCOL)]
        got.append(send(jnp.where(sends_low, low, top), pairs))
    for moves, block in zip(RING[step], got):
        top = jnp.where(among(row, [t for _, t, panel in moves if panel == 0]), block, top)
        low = jnp.where(among(row, [t for _, t, panel in moves if panel == 1]), block, low)
    return top, low


def tree():
    along = {"z": lambda h, k: (h[0] + k, h[1], h[2]), "y": lambda h, k: (h[0], h[1] + k, h[2])}
    along["x"] = lambda h, k: (h[0], h[1], h[2] + k)
    far, near, side = ("z", (8, 4, 12)), ("z", (2, 1, 15)), (2, 1, 3)
    orders = ((far, near, ("y", side), ("x", side)), (("y", side), ("x", side), far, near))
    held = [[(0, 0, 0)], [(1, 0, 0)]]
    levels = []
    for level in range(4):
        sets = [[], [], []]
        for half, order in enumerate(orders):
            axis, offsets = order[level]
            new = []
            for n, k in enumerate(offsets):
                for h in held[half]:
                    t = along[axis](h, k)
                    sets[n].append((device(*h, half), device(*t, half)))
                    new.append(t)
            held[half] = held[half] + new
        levels.append(sets)
    return levels


CHIPS = [(z, y, x) for z in range(NZ) for y in range(NY) for x in range(NX)]


SWAP = [(device(*h, c), device(*h, 1 - c)) for h in CHIPS for c in range(NC)]


def shards(matrix):
    row = lax.axis_index("row")
    col = lax.axis_index("col")
    me = row * NCOL + col
    core = col % NC
    a_count, width, c_count, _ = matrix.shape

    y, x = col // (NX * NC), col // NC % NX
    hold = lax.optimization_barrier

    def step_panels(step, state):
        with jax.named_scope("spread_panels"):
            first, second, top, low = state
            return spread_rows(step, first, second, y, x) + spread_cols(step, top, low, row)

    def step_diagonal(half, sets):
        with jax.named_scope("spread_diagonal"):
            got = [send(half, pairs) for pairs in sets]
            return half + (got[0] + got[1] + got[2])

    panels = matrix[:2, :, 0, :], matrix[2:, :, 0, :], matrix[0], matrix[0]
    with jax.named_scope("spread_diagonal"):
        corner = matrix[0, :, 0, :]
        upper, lower = corner[:TILE], corner[TILE:]
        roots = device(0, 0, 0, 0), device(1, 0, 0, 1)
        across = device(1, 0, 0, 0)
        beside = jnp.stack((upper[:, :TILE], upper[:, TILE:])), jnp.stack((lower[:, :TILE], lower[:, TILE:]))
        got = send(beside[0], [(across, roots[0])]) + send(beside[1], [(across, roots[1])])
        half = jnp.concatenate((jnp.stack((upper[:, :TILE], lower[:, :TILE], lower[:, TILE:])), got))
        half = only((me == roots[0]) | (me == roots[1]), half)
    levels = tree()
    half, panels = hold((step_diagonal(step_diagonal(half, levels[0]), levels[1]), step_panels(0, panels)))
    half = step_diagonal(step_diagonal(half, levels[2]), levels[3])
    with jax.named_scope("spread_diagonal"):
        other = send(half, SWAP)
        diagonal = jnp.where(core == 0, half, other), jnp.where(core == 0, other, half)
    diagonal, panels = hold((diagonal, step_panels(1, panels)))
    with jax.named_scope("factor_diagonal"):
        inverse = factor(*diagonal)
    inverse, panels = hold((inverse, step_panels(2, panels)))
    first, second, top, low = hold(step_panels(3, panels))
    with jax.named_scope("spread_panels"):
        mine = jnp.concatenate((first, second))
        other = send(mine, SWAP)
        left = jnp.where(core == 1, other, mine)
        right = jnp.where(core == 1, mine, other)
    with jax.named_scope("update"):
        left = left.reshape(a_count * width, width)
        right = right.reshape(a_count * width, width)
        head = dot(left, inverse[:width, :width], 1, 1)
        tail = dot(left, inverse[width:, :width], 1, 1) + dot(right, inverse[width:, width:], 1, 1)
        rows = jnp.concatenate((head, tail), 1).reshape(a_count, width, 2 * width)
        top, low = (part.reshape(width, c_count * width) for part in (top, low))
        solved = dot(inverse[:, :width], top, 1, 0) + dot(inverse[:, width:], low, 1, 0)
        solved = solved.reshape(2 * width, c_count, width)
        product = jnp.einsum("apk,kcq->apcq", rows, solved, precision=HI)
        row_ids = (jnp.arange(a_count, dtype=jnp.int32) * NZ + row)[:, None, None]
        col_ids = (jnp.arange(c_count, dtype=jnp.int32) * NCOL + col)[None, None, :, None]
        p = lax.broadcasted_iota(jnp.int32, (1, width, width), 1)
        q = lax.broadcasted_iota(jnp.int32, (1, width, width), 2)
        lower = p >= q
        head = head.reshape(a_count, width, width)
        tail = tail.reshape(a_count, width, width)
        head = jnp.where((row_ids > 0) | lower, head, 0.0)
        tail = jnp.where((row_ids > 1) | ((row_ids == 1) & lower), tail, 0.0)
        trailing = jnp.where(row_ids[..., None] > 1, matrix - product, 0.0)
        return jnp.where(
            col_ids == 0, head[:, :, None, :], jnp.where(col_ids == 1, tail[:, :, None, :], trailing)
        )


def solution(mesh):
    spec = (P(None, "row", None, "col"),)
    return jax.shard_map(shards, mesh=mesh, in_specs=spec, out_specs=spec[0], check_vma=False)
```

```python
import jax
import jax.numpy as jnp
from jax import lax
from jax.experimental import pallas as pl
from jax.experimental.pallas import tpu as pltpu
from jax.sharding import PartitionSpec as P

HI = lax.Precision.HIGHEST
TILE = 128
STEP = 32
SUB = 16
NZ, NY, NX, NC = 16, 4, 4, 2
NCOL = NY * NX * NC
TILES = (((0, 0), (1, 0), (1, 1), (2, 0), (2, 1)), ((2, 2), (3, 2), (3, 3), (3, 0), (3, 1)))
HALF = len(TILES[0])


def dot(a, b, ca, cb):
    dims = (((ca,), (cb,)), ((), ()))
    return lax.dot_general(a, b, dims, precision=HI, preferred_element_type=jnp.float32)


def factor_tile(work):
    lane = lax.broadcasted_iota(jnp.int32, (SUB, 2 * TILE), 1)
    sub = lax.broadcasted_iota(jnp.int32, (SUB, 2 * TILE), 0)
    for start in range(0, TILE, STEP):
        stop = start + STEP
        parts = [work[s : s + SUB, :] for s in range(start, stop, SUB)]
        for p in range(STEP // SUB):
            first = start + p * SUB
            rows = parts[p]
            columns = [jnp.broadcast_to(rows[:, first + j : first + j + 1], (SUB, TILE)) for j in range(SUB)]
            below = [
                [jnp.broadcast_to(r[:, first + j : first + j + 1], (SUB, TILE)) for j in range(SUB)]
                for r in parts[p + 1 :]
            ]
            done = jnp.zeros_like(rows)
            for j in range(SUB):
                scale = lax.rsqrt(columns[j][j : j + 1, :])
                weight = columns[j] * scale
                row = rows[j : j + 1, :] * jnp.concatenate((scale, scale), 1)
                rows = rows - jnp.concatenate((weight, weight), 1) * row
                for t, cols in enumerate(below):
                    w = cols[j] * scale
                    parts[p + 1 + t] = parts[p + 1 + t] - jnp.concatenate((w, w), 1) * row
                    for i in range(j + 1, SUB):
                        cols[i] = cols[i] - w * (columns[i][j : j + 1, :] * scale)
                for i in range(j + 1, SUB):
                    columns[i] = columns[i] - weight * (columns[i][j : j + 1, :] * scale)
                done = jnp.where(sub == j, row, done)
            parts[p] = jnp.where(lane >= first + sub, done, 0.0)
        done = jnp.concatenate(parts)
        work[start:stop, :] = done
        if stop < TILE:
            work[stop:, :] = work[stop:, :] - dot(done[:, stop:TILE], done, 0, 0)


def factor_kernel(first, second, inv, a, work):
    n = inv.shape[0]
    for block, places in zip((first, second), TILES):
        for t, (i, j) in enumerate(places):
            a[i * TILE : (i + 1) * TILE, j * TILE : (j + 1) * TILE] = block[t]
    ri = lax.broadcasted_iota(jnp.int32, (TILE, TILE), 0)
    ci = lax.broadcasted_iota(jnp.int32, (TILE, TILE), 1)
    eye = jnp.where(ri == ci, 1.0, 0.0)
    inv[...] = jnp.zeros_like(inv)
    for s in range(0, n, TILE):
        e = s + TILE
        work[:, :TILE] = a[s:e, s:e]
        work[:, TILE:] = eye
        factor_tile(work)
        tile_inv = work[:, TILE:]
        if s:
            inv[s:e, 0:s] = dot(tile_inv, inv[s:e, 0:s], 1, 0)
        inv[s:e, s:e] = tile_inv
        if e < n:
            panel = dot(a[e:, s:e], tile_inv, 1, 1)
            for r in range(e, n, TILE):
                rows = panel[r - e : r - e + TILE]
                a[r : r + TILE, e : r + TILE] = a[r : r + TILE, e : r + TILE] - dot(
                    rows, panel[: r - e + TILE], 1, 1
                )
            inv[e:, 0:e] = inv[e:, 0:e] - dot(panel, inv[s:e, 0:e], 1, 0)


def factor(first, second):
    n = 4 * TILE
    vmem = pl.BlockSpec(memory_space=pltpu.VMEM)
    return pl.pallas_call(
        factor_kernel,
        out_shape=jax.ShapeDtypeStruct((n, n), jnp.float32),
        in_specs=[vmem] * 2,
        out_specs=vmem,
        scratch_shapes=[pltpu.VMEM((n, n), jnp.float32), pltpu.VMEM((TILE, 2 * TILE), jnp.float32)],
        compiler_params=pltpu.CompilerParams(vmem_limit_bytes=24 * 1024 * 1024),
        cost_estimate=pl.CostEstimate(flops=30_000_000_000, bytes_accessed=2_000_000, transcendentals=0),
    )(first, second)


def device(z, y, x, c):
    return (((z % NZ) * NY + y % NY) * NX + x % NX) * NC + c


def send(block, pairs):
    return lax.ppermute(block, ("row", "col"), pairs)


def only(mask, block):
    return jnp.where(mask, block, jnp.zeros_like(block))


def plane(pairs):
    return [(device(z, *s, c), device(z, *t, c)) for z in range(NZ) for s, t in pairs for c in range(NC)]


def spread_rows(step, first, second, y, x):
    k = (2, 1, 2, 1)[step]
    spots = range(0, NY, 2 * k)
    if step < 2:
        to_first = send(first, plane([((y, 0), (y + k, 0)) for y in spots]))
        to_second = send(second, plane([((0, x), (0, x + k)) for x in spots]))
    else:
        to_first = send(first, plane([((y, x), (y, x + k)) for y in range(NY) for x in spots]))
        to_second = send(second, plane([((y, x), (y + k, x)) for y in spots for x in range(NX)]))
    lead, other = (y, x), (x, y)
    at = [(m if step < 2 else n) % (2 * k) == k for m, n in (lead, other)]
    if step < 2:
        at = [at[0] & (x == 0), at[1] & (y == 0)]
    return jnp.where(at[0], to_first, first), jnp.where(at[1], to_second, second)


RING = (
    (((0, 11, 0), (1, 6, 1)), ((0, 1, 0), (1, 0, 1))),
    (((0, 11, 1), (1, 6, 0), (11, 14, 0), (6, 3, 1)), ((11, 9, 0), (6, 8, 1))),
    (
        ((0, 14, 1), (14, 15, 0), (9, 10, 0), (8, 9, 1), (11, 12, 0), (1, 3, 0), (3, 2, 1), (6, 7, 0)),
        ((14, 13, 0), (9, 8, 0), (8, 7, 1), (11, 10, 1), (3, 4, 1), (6, 5, 0)),
    ),
    (((0, 15, 1), (14, 13, 1), (11, 12, 1), (1, 2, 0), (3, 4, 0), (6, 5, 1)),),
)


def among(index, values):
    found = jnp.zeros((), bool)
    for value in values:
        found |= index == value
    return found


def spread_cols(step, top, low, row):
    got = []
    for moves in RING[step]:
        sends_low = among(row, [s for s, _, panel in moves if panel == 1])
        pairs = [(s * NCOL + j, t * NCOL + j) for s, t, _ in moves for j in range(NCOL)]
        got.append(send(jnp.where(sends_low, low, top), pairs))
    for moves, block in zip(RING[step], got):
        top = jnp.where(among(row, [t for _, t, panel in moves if panel == 0]), block, top)
        low = jnp.where(among(row, [t for _, t, panel in moves if panel == 1]), block, low)
    return top, low


def tree():
    along = {"z": lambda h, k: (h[0] + k, h[1], h[2]), "y": lambda h, k: (h[0], h[1] + k, h[2])}
    along["x"] = lambda h, k: (h[0], h[1], h[2] + k)
    far, near, side = ("z", (8, 4, 12)), ("z", (2, 1, 15)), (2, 1, 3)
    orders = ((far, near, ("y", side), ("x", side)), (("y", side), far, ("x", side), near))
    held = [[(0, 0, 0)], [(1, 0, 0)]]
    levels = []
    for level in range(4):
        sets = [[], [], []]
        for half, order in enumerate(orders):
            axis, offsets = order[level]
            new = []
            for n, k in enumerate(offsets):
                for h in held[half]:
                    t = along[axis](h, k)
                    sets[n].append((device(*h, half), device(*t, half)))
                    new.append(t)
            held[half] = held[half] + new
        levels.append(sets)
    return levels


CHIPS = [(z, y, x) for z in range(NZ) for y in range(NY) for x in range(NX)]


SWAP = [(device(*h, c), device(*h, 1 - c)) for h in CHIPS for c in range(NC)]


def shards(matrix):
    row = lax.axis_index("row")
    col = lax.axis_index("col")
    me = row * NCOL + col
    core = col % NC
    a_count, width, c_count, _ = matrix.shape

    y, x = col // (NX * NC), col // NC % NX
    hold = lax.optimization_barrier

    def step_panels(step, state):
        with jax.named_scope("spread_panels"):
            first, second, top, low = state
            return spread_rows(step, first, second, y, x) + spread_cols(step, top, low, row)

    def step_diagonal(half, sets):
        with jax.named_scope("spread_diagonal"):
            got = [send(half, pairs) for pairs in sets]
            return half + (got[0] + got[1] + got[2])

    panels = matrix[:2, :, 0, :], matrix[2:, :, 0, :], matrix[0], matrix[0]
    with jax.named_scope("spread_diagonal"):
        corner = matrix[0, :, 0, :]
        upper, lower = corner[:TILE], corner[TILE:]
        roots = device(0, 0, 0, 0), device(1, 0, 0, 1)
        across = device(1, 0, 0, 0)
        beside = jnp.stack((upper[:, :TILE], upper[:, TILE:])), jnp.stack((lower[:, :TILE], lower[:, TILE:]))
        got = send(beside[0], [(across, roots[0])]) + send(beside[1], [(across, roots[1])])
        half = jnp.concatenate((jnp.stack((upper[:, :TILE], lower[:, :TILE], lower[:, TILE:])), got))
        half = only((me == roots[0]) | (me == roots[1]), half)
    levels = tree()
    half, panels = hold((step_diagonal(step_diagonal(half, levels[0]), levels[1]), step_panels(0, panels)))
    half = step_diagonal(step_diagonal(half, levels[2]), levels[3])
    with jax.named_scope("spread_diagonal"):
        other = send(half, SWAP)
        diagonal = jnp.where(core == 0, half, other), jnp.where(core == 0, other, half)
    diagonal, panels = hold((diagonal, step_panels(1, panels)))
    with jax.named_scope("factor_diagonal"):
        inverse = factor(*diagonal)
    inverse, panels = hold((inverse, step_panels(2, panels)))
    first, second, top, low = hold(step_panels(3, panels))
    with jax.named_scope("spread_panels"):
        mine = jnp.concatenate((first, second))
        other = send(mine, SWAP)
        left = jnp.where(core == 1, other, mine)
        right = jnp.where(core == 1, mine, other)
    with jax.named_scope("update"):
        left = left.reshape(a_count * width, width)
        right = right.reshape(a_count * width, width)
        head = dot(left, inverse[:width, :width], 1, 1)
        tail = dot(left, inverse[width:, :width], 1, 1) + dot(right, inverse[width:, width:], 1, 1)
        rows = jnp.concatenate((head, tail), 1).reshape(a_count, width, 2 * width)
        top, low = (part.reshape(width, c_count * width) for part in (top, low))
        solved = dot(inverse[:, :width], top, 1, 0) + dot(inverse[:, width:], low, 1, 0)
        solved = solved.reshape(2 * width, c_count, width)
        product = jnp.einsum("apk,kcq->apcq", rows, solved, precision=HI)
        row_ids = (jnp.arange(a_count, dtype=jnp.int32) * NZ + row)[:, None, None]
        col_ids = (jnp.arange(c_count, dtype=jnp.int32) * NCOL + col)[None, None, :, None]
        p = lax.broadcasted_iota(jnp.int32, (1, width, width), 1)
        q = lax.broadcasted_iota(jnp.int32, (1, width, width), 2)
        lower = p >= q
        head = head.reshape(a_count, width, width)
        tail = tail.reshape(a_count, width, width)
        head = jnp.where((row_ids > 0) | lower, head, 0.0)
        tail = jnp.where((row_ids > 1) | ((row_ids == 1) & lower), tail, 0.0)
        trailing = jnp.where(row_ids[..., None] > 1, matrix - product, 0.0)
        return jnp.where(
            col_ids == 0, head[:, :, None, :], jnp.where(col_ids == 1, tail[:, :, None, :], trailing)
        )


def solution(mesh):
    spec = (P(None, "row", None, "col"),)
    return jax.shard_map(shards, mesh=mesh, in_specs=spec, out_specs=spec[0], check_vma=False)
```
